32 devices in a mesh: sec: 2 (over x), row: 4 (over z), col: 4 (over y, core).
Axes of the slice: x: 2, y: 2, z: 4, core: 2. Of those that a mesh axis runs over, the one named last changes fastest.
Arguments:
- held_inverse: bfloat16 [12288, 12288], P('row', ('sec', 'col')), as said below
- factor_panels: bfloat16 [2, 12288, 1024], P(None, ('sec', 'col'), 'row'), may hold values from -0.125 to 0.125
- block_inverses: bfloat16 [2, 1024, 1024], P(None, 'row'), as said below
- covariance: float32 [12288, 12288], P('row', ('sec', 'col')), may hold values from -0.9 to 0.9
Outputs:
- updated: float32 [12288, 12288], P('row', ('sec', 'col'))
The draws below stay inside these ranges and needn't reach their ends.
Inputs may be any that keep to these rules, and one draw needn't show every extreme that they name: held_inverse is lower triangular with a positive diagonal. Each block of block_inverses is lower triangular with a positive diagonal.
All inputs are finite; a program needn't handle non-finite values.
Results may differ from the reference program's by a relative error of at most 0.0038.
Values may be sent and summed in bfloat16 or wider, within the bound.
No kernel may reach another device: no remote copies, remote signals or barrier semaphores. Data moves between devices by JAX's collectives and lax.ppermute only.
A program may use at most 128 MiB of HBM per device.

```python
import jax
import jax.numpy as jnp
from jax import lax

M = 12288
B = 1024
PANELS = 2


def draw_held_inverse(key, part):
    first, second = jax.random.split(jax.random.fold_in(key, 11), 2)
    lower = jax.random.normal(first, (M, M), jnp.float32) * (1.5 / jnp.sqrt(M * 1.0))
    diagonal = jax.random.uniform(second, (M,), jnp.float32, 0.6, 1.6)
    return (jnp.tril(lower, -1) + jnp.diag(diagonal)).astype(jnp.bfloat16)


def draw_block_inverses(key, part):
    first, second = jax.random.split(jax.random.fold_in(key, 23))
    lower = jax.random.normal(first, (PANELS, B, B), jnp.float32) / jnp.sqrt(B * 1.0)
    diagonal = jax.random.uniform(second, (PANELS, B), jnp.float32, 0.5, 2.0)
    eye = jnp.eye(B, dtype=jnp.float32)
    return (jnp.tril(lower, -1) + diagonal[:, :, None] * eye[None]).astype(jnp.bfloat16)


def levels(rng, extent, shards, low, top_value):
    level, own = 1.0, jax.random.fold_in(rng, 6)
    for position, parts in shards:
        steps = jnp.exp(jax.random.uniform(jax.random.fold_in(own, position), (parts,), jnp.float32, low / len(shards), top_value / len(shards)))
        level = level * jnp.repeat(steps, extent[position] // parts).reshape([-1 if axis == position else 1 for axis in range(len(extent))])
    return level


def normal_values(rng, shape, scale, limit, pieces=(), kind=jnp.bfloat16):
    array = jax.random.normal(rng, shape, jnp.float32) * scale
    if len(pieces) > 0:
        array = levels(rng, shape, pieces, -0.22, 0.18) * array
    return jnp.clip(array, min=-limit, max=limit).astype(kind)


def setup_inputs(seed: int = 0) -> dict:
    arg_keys = jax.random.split(jax.random.key(seed), 5)
    held_inverse = draw_held_inverse(jax.random.fold_in(arg_keys[4], 71), 0)
    factor_panels = normal_values(arg_keys[1], (PANELS, M, B), (B * PANELS) ** -0.5, 0.125, ((1, 8), (2, 4)))
    block_inverses = draw_block_inverses(jax.random.fold_in(arg_keys[4], 71), 0)
    covariance = normal_values(arg_keys[3], (M, M), 0.15, 0.9, ((0, 4), (1, 8)), jnp.float32)
    return {"held_inverse": held_inverse, "factor_panels": factor_panels, "block_inverses": block_inverses, "covariance": covariance}


def reference(held_inverse, factor_panels, block_inverses, covariance):
    total = covariance
    for panel in range(PANELS):
        scaled = jnp.dot(factor_panels[panel], block_inverses[panel], preferred_element_type=jnp.float32).astype(jnp.bfloat16)
        inverse = (-jnp.dot(held_inverse, scaled, preferred_element_type=jnp.float32)).astype(jnp.bfloat16)
        total = total + lax.dot_general(inverse, inverse, (((1,), (1,)), ((), ())), preferred_element_type=jnp.float32)
    return total
```

```python
import jax
import jax.numpy as jnp
from jax import lax
from jax.sharding import PartitionSpec as P

AXES = ("sec", "row", "col")
SUBS = 1


def pick(array, index):
    return lax.dynamic_index_in_dim(array, index, 0, keepdims=False)


def make_body(shape):
    secs, rows, cols = (shape[axis] for axis in AXES)
    mates = secs * cols // rows
    lanes = cols // mates
    swaps = secs == lanes
    sizes = (secs, lanes)

    def send(value, route):
        pairs = []
        for s in range(secs):
            for r in range(rows):
                for y in range(lanes):
                    for k in range(mates):
                        to = route(s, r, y, k)
                        if to is not None:
                            t, q, v, m = to
                            source = (s * rows + r) * cols + y * mates + k
                            pairs.append((source, (t * rows + q) * cols + v * mates + m))
        return lax.ppermute(value, AXES, pairs)

    def to_mate(value, step):
        return send(value, lambda s, r, y, k: (s, r, y, (k + step) % mates))

    def to_plane(value, phase, step):
        def route(s, r, y, k):
            along_sec = phase == (1 if swaps and k % 2 else 0)
            if along_sec:
                return ((s + step) % secs, r, y, k)
            return (s, r, (y + step) % lanes, k)

        return send(value, route)

    def row_gather(value, wanted):
        ups, downs = [], []
        up = down = value
        for t in range(1, rows):

            def upward(s, r, y, k, t=t):
                return (s, r + 1, y, k) if r + 1 < rows and r + 1 - t >= 0 else None

            def downward(s, r, y, k, t=t):
                ok = r >= 1 and r - 1 + t < rows and wanted(r - 1, s * lanes + y)
                return (s, r - 1, y, k) if ok else None

            up, down = send(up, upward), send(down, downward)
            ups.append(up)
            downs.append(down)
        return ups, downs

    def body(held_inverse, factor_panels, block_inverses, covariance):
        panels, tile, depth = factor_panels.shape
        width = block_inverses.shape[2]
        sec, row = lax.axis_index("sec"), lax.axis_index("row")
        lane, mate = lax.axis_index("col") // mates, lax.axis_index("col") % mates
        block = sec * lanes + lane
        piece = tile // (secs * lanes)
        sub = piece // SUBS

        def first_second(mate):
            if not swaps:
                return sec, lane
            odd = mate % 2 == 1
            return jnp.where(odd, lane, sec), jnp.where(odd, sec, lane)

        def piece_of(mate, one, two):
            if not swaps:
                return one * lanes + two
            return jnp.where(mate % 2 == 1, two * lanes + one, one * lanes + two)

        def below(ups, downs, t):
            return jnp.where(row >= t, ups[t - 1], downs[rows - t - 1])

        part = block_inverses.shape[1] // (mates * rows)
        group = block * mates + mate
        slice_ = lax.dynamic_slice_in_dim(block_inverses, group * part, part, 1)
        ups, downs = row_gather(slice_, lambda r, q: True)
        slices = jnp.stack([slice_] + [below(ups, downs, t) for t in range(1, rows)], 1)
        inverses = []
        for panel in range(panels):
            order = (0, 1) if panel % 2 == 0 else (1, 0)

            def shifted(value, axis, step):
                if axis == 0:
                    return send(value, lambda s, r, y, k: ((s + step) % secs, r, y, k))
                return send(value, lambda s, r, y, k: (s, r, (y + step) % lanes, k))

            found = {(0, 0): slices[panel]}
            for axis in order:
                for at, value in list(found.items()):
                    for step in range(1, sizes[axis]):
                        key = (step, at[1]) if axis == 0 else (at[0], step)
                        found[key] = shifted(value, axis, step)
            whole = jnp.zeros((rows, secs * lanes * mates, part, width), jnp.bfloat16)
            mine = jnp.zeros((rows, secs * lanes, part, width), jnp.bfloat16)
            for (ds, dy), value in found.items():
                at = (sec - ds) % secs * lanes + (lane - dy) % lanes
                mine = lax.dynamic_update_slice(mine, value[:, None], (0, at, 0, 0))
            whole = whole.reshape(rows, secs * lanes, mates, part, width)
            for step in range(mates):
                value = mine if step == 0 else to_mate(mine, step)
                whole = lax.dynamic_update_slice(
                    whole, value[:, :, None], (0, 0, (mate - step) % mates, 0, 0)
                )
            inverses.append(whole.reshape(rows * depth, width))

        halves = held_inverse.reshape(mates, secs * lanes, piece, tile)

        def share(step):
            target = (mate + step) % mates
            half = pick(halves, target)
            one, two = first_second(target)
            n1, n2 = sizes
            parts = [
                pick(half, piece_of(target, (one + a) % n1, (two + b) % n2)).reshape(SUBS, sub, tile)
                for a in range(n1)
                for b in range(n2)
            ]
            return jnp.stack(parts, 1)

        held = [share(0)] + [to_mate(share(step), step) for step in range(1, mates)]

        one, two = first_second(mate)
        n1, n2 = sizes
        total = covariance
        gathered = [
            row_gather(factor_panels[panel], lambda r, q: r >= q) for panel in range(panels)
        ]
        for panel in range(panels):
            ups, downs = gathered[panel]
            factor = jnp.concatenate(
                [factor_panels[panel]] + [below(ups, downs, t) for t in range(1, rows)], 1
            )
            scaled = jnp.dot(
                factor, inverses[panel], preferred_element_type=jnp.float32
            ).astype(jnp.bfloat16)
            scaleds = [scaled] + [to_mate(scaled, step) for step in range(1, mates)]
            row_buffer = jnp.zeros((mates, secs * lanes, piece, width), jnp.bfloat16)
            col_buffer = jnp.zeros((secs * lanes, piece, width), jnp.bfloat16)
            for index in range(SUBS):
                terms = sum(
                    jnp.dot(
                        held[step][index].reshape(n1 * n2 * sub, tile),
                        scaleds[step],
                        preferred_element_type=jnp.float32,
                    )
                    for step in range(mates)
                ).reshape(n1, n2, sub, width)
                half_sum = terms[0]
                for step in range(1, n1):
                    half_sum = half_sum + to_plane(terms[step].astype(jnp.bfloat16), 0, step)
                whole_sum = half_sum[0]
                for step in range(1, n2):
                    whole_sum = whole_sum + to_plane(half_sum[step].astype(jnp.bfloat16), 1, step)
                own = whole_sum.astype(jnp.bfloat16)

                found = {(0, 0): own}
                for a in range(1, n1):
                    found[a, 0] = to_plane(own, 0, a)
                for a in range(n1):
                    for b in range(1, n2):
                        found[a, b] = to_plane(found[a, 0], 1, b)
                places = {
                    key: piece_of(mate, (one - key[0]) % n1, (two - key[1]) % n2) for key in found
                }
                for key, value in found.items():
                    row_buffer = lax.dynamic_update_slice(
                        row_buffer, value[None, None], (mate, places[key], index * sub, 0)
                    )

                ups, downs = row_gather(own, lambda r, q: True)
                arrived = {}
                for ds in range(secs):
                    for dy in range(lanes):
                        target = (sec + ds) % secs * lanes + (lane + dy) % lanes
                        sums = []
                        for t in range(1, rows):
                            value = jnp.where(row - t == target, ups[t - 1], downs[t - 1])
                            if ds == 0 and dy == 0:
                                value = jnp.where(abs(row - target) == t, value, 0)
                            else:

                                def route(s, r, y, k, t=t):
                                    v, w = (s + ds) % secs, (y + dy) % lanes
                                    return (v, r, w, k) if abs(r - v * lanes - w) == t else None

                                value = send(value, route)
                            sums.append(value)
                        arrived[ds, dy] = sum(sums[1:], sums[0])
                for (ds, dy), value in arrived.items():
                    place = (sec - ds) % secs * lanes + (lane - dy) % lanes
                    col_buffer = lax.dynamic_update_slice(
                        col_buffer, value[None], (place, index * sub, 0)
                    )
            own_half = pick(row_buffer, mate)
            for step in range(1, mates):
                row_buffer = lax.dynamic_update_slice(
                    row_buffer, to_mate(own_half, step)[None], ((mate - step) % mates, 0, 0, 0)
                )
            columns = jnp.where(row == block, own_half, col_buffer)
            total = total + lax.dot_general(
                row_buffer.reshape(-1, width),
                columns.reshape(-1, width),
                (((1,), (1,)), ((), ())),
                preferred_element_type=jnp.float32,
            )
        return total

    return body


def solution(mesh):
    in_specs = (
        P("row", ("sec", "col")),
        P(None, ("sec", "col"), "row"),
        P(None, "row", None),
        P("row", ("sec", "col")),
    )
    out_specs = P("row", ("sec", "col"))
    return jax.shard_map(
        make_body(dict(mesh.shape)), mesh=mesh, in_specs=in_specs, out_specs=out_specs, check_vma=False
    )
```

```python
import jax
import jax.numpy as jnp
from jax import lax
from jax.experimental import pallas as pl
from jax.experimental.pallas import tpu as pltpu
from jax.sharding import PartitionSpec as P

AXES = ("sec", "row", "col")


def pick(array, index):
    return lax.dynamic_index_in_dim(array, index, 0, keepdims=False)


def make_body(shape):
    secs, rows, cols = (shape[axis] for axis in AXES)
    mates = secs * cols // rows
    lanes = cols // mates
    swaps = secs == lanes
    sizes = (secs, lanes)
    steps = [(ds, dy) for dy in range(lanes) for ds in range(secs) if ds or dy]

    def send(value, route, name):
        pairs = []
        for s in range(secs):
            for r in range(rows):
                for y in range(lanes):
                    for k in range(mates):
                        to = route(s, r, y, k)
                        if to is not None:
                            t, q, v, m = to
                            source = (s * rows + r) * cols + y * mates + k
                            pairs.append((source, (t * rows + q) * cols + v * mates + m))
        with jax.named_scope(name):
            return lax.ppermute(value, AXES, pairs)

    def to_mate(value, step, name):
        return send(value, lambda s, r, y, k: (s, r, y, (k + step) % mates), name)

    def to_plane(value, phase, step, name):
        def route(s, r, y, k):
            along_sec = phase == (1 if swaps and k % 2 else 0)
            if along_sec:
                return ((s + step) % secs, r, y, k)
            return (s, r, (y + step) % lanes, k)

        return send(value, route, name)

    free = pl.CostEstimate(flops=0, bytes_accessed=0, transcendentals=0)
    params = pltpu.CompilerParams(vmem_limit_bytes=40 * 2**20)

    def scale(factor, inverse):
        _, tile, depth = factor.shape
        full, width = inverse.shape
        chunk = tile // rows

        def kernel(factor_ref, inverse_ref, out_ref):
            out_ref[...] = jnp.dot(
                jnp.concatenate([factor_ref[i] for i in range(rows)], 1),
                inverse_ref[...],
                preferred_element_type=jnp.float32,
            ).astype(out_ref.dtype)

        return pl.pallas_call(
            kernel,
            out_shape=jax.ShapeDtypeStruct((tile, width), factor.dtype),
            grid=(tile // chunk,),
            in_specs=[
                pl.BlockSpec((rows, chunk, depth), lambda i: (0, i, 0)),
                pl.BlockSpec((full, width), lambda i: (0, 0)),
            ],
            out_specs=pl.BlockSpec((chunk, width), lambda i: (i, 0)),
            compiler_params=params,
            cost_estimate=free,
        )(factor, inverse)

    def product(held, scaleds, first, count, piece, kind):
        tile, width = scaleds[0].shape

        def kernel(*refs):
            left, right, out_ref = refs[:mates], refs[mates:-1], refs[-1]
            total = jnp.dot(left[0][...], right[0][...], preferred_element_type=jnp.float32)
            for step in range(1, mates):
                total += jnp.dot(
                    left[step][...], right[step][...], preferred_element_type=jnp.float32
                )
            out_ref[...] = total.astype(out_ref.dtype)

        offset = first // piece
        return pl.pallas_call(
            kernel,
            out_shape=jax.ShapeDtypeStruct((count, width), kind),
            grid=(count // piece,),
            in_specs=[pl.BlockSpec((piece, tile), lambda i: (i + offset, 0))] * mates
            + [pl.BlockSpec((tile, width), lambda i: (0, 0))] * mates,
            out_specs=pl.BlockSpec((piece, width), lambda i: (i, 0)),
            compiler_params=params,
            cost_estimate=free,
        )(*held, *scaleds)

    def update(meta, total, lefts, own, came):
        n1, piece, width = lefts[0].shape
        height, tile = total.shape
        n_left = len(lefts) * n1
        operands = [*lefts, own, *came]

        def kernel(meta_ref, total_ref, *refs):
            out_ref, left_buf, right_buf, left_sem, right_sem = refs[-5:]
            refs = list(refs[:-5])
            take = lambda n: [refs.pop(0) for _ in range(n)]
            left, (own_ref,) = take(len(lefts)), take(1)
            arrived = take(len(came))
            gap, mate = meta_ref[0], meta_ref[1]
            at = 2 + n_left + rows

            def left_copy(i):
                source = left[i // n1].at[i % n1]
                return pltpu.make_async_copy(source, left_buf.at[meta_ref[2 + i]], left_sem.at[i])

            def right_copy(j, source, place):
                rows_at = pl.ds(pl.multiple_of(place * piece, piece), piece)
                return pltpu.make_async_copy(source, right_buf.at[rows_at], right_sem.at[j])

            @pl.when(pl.program_id(0) == 0)
            def _():
                for j in range(rows):
                    place = meta_ref[2 + n_left + j]

                    @pl.when(gap == 0)
                    def _():
                        source = left[j // n1].at[j % n1]
                        right_copy(j, source, meta_ref[2 + j] - mate * rows).start()

                    @pl.when(gap != 0)
                    def _():
                        source = arrived[j - 1] if j else own_ref.at[meta_ref[at]]
                        right_copy(j, source, place).start()

                for i in range(n_left):
                    left_copy(i).start()
                for j in range(rows):
                    right_copy(j, left[0].at[0], 0).wait()
                for i in range(n_left):
                    left_copy(i).wait()

            out_ref[...] = total_ref[...] + lax.dot_general(
                left_buf[pl.program_id(0)],
                right_buf[...],
                (((1,), (1,)), ((), ())),
                preferred_element_type=jnp.float32,
            )

        block = pl.BlockSpec((piece, tile), lambda i, meta_ref: (i, 0))
        return pl.pallas_call(
            kernel,
            out_shape=jax.ShapeDtypeStruct(total.shape, total.dtype),
            grid_spec=pltpu.PrefetchScalarGridSpec(
                num_scalar_prefetch=1,
                grid=(n_left,),
                in_specs=[block] + [pl.BlockSpec(memory_space=pl.ANY)] * len(operands),
                out_specs=block,
                scratch_shapes=[
                    pltpu.VMEM((n_left, piece, width), jnp.bfloat16),
                    pltpu.VMEM((tile, width), jnp.bfloat16),
                    pltpu.SemaphoreType.DMA((n_left,)),
                    pltpu.SemaphoreType.DMA((rows,)),
                ],
            ),
            compiler_params=params,
            cost_estimate=pl.CostEstimate(
                flops=2 * height * tile * width,
                bytes_accessed=8 * height * tile + 2 * width * (height + tile),
                transcendentals=0,
            ),
        )(meta, total, *operands)

    def body(held_inverse, factor_panels, block_inverses, covariance):
        panels, tile, depth = factor_panels.shape
        sec, row = lax.axis_index("sec"), lax.axis_index("row")
        lane, mate = lax.axis_index("col") // mates, lax.axis_index("col") % mates
        block = sec * lanes + lane
        piece = tile // (secs * lanes)
        n1, n2 = sizes

        def first_second(mate):
            if not swaps:
                return sec, lane
            odd = mate % 2 == 1
            return jnp.where(odd, lane, sec), jnp.where(odd, sec, lane)

        def piece_of(mate, one, two):
            if not swaps:
                return one * lanes + two
            return jnp.where(mate % 2 == 1, two * lanes + one, one * lanes + two)

        def fence(*values):
            return lax.optimization_barrier(values)

        halves = held_inverse.reshape(mates, secs * lanes, piece, tile)

        def share(step):
            target = (mate + step) % mates
            half = pick(halves, target)
            one, two = first_second(target)
            return jnp.concatenate(
                [
                    pick(half, piece_of(target, (one + a) % n1, (two + b) % n2))
                    for a in range(n1)
                    for b in range(n2)
                ]
            )

        def whole_inverse(stack, name):
            part_rows = stack[None]
            for phase, size in enumerate(sizes):
                kept = part_rows
                for step in range(1, size):
                    moved = to_plane(kept, phase, step, f"{name}_plane{phase}")
                    part_rows = jnp.concatenate([part_rows, moved])
            kept = part_rows
            for step in range(1, mates):
                part_rows = jnp.concatenate([part_rows, to_mate(kept, step, f"{name}_swap")])
            ordered = []
            for q in range(rows):
                for k in range(mates):
                    one, two = first_second(k)
                    at_one, at_two = q // lanes, q % lanes
                    if swaps and k % 2:
                        at_one, at_two = at_two, at_one
                    index = (one - at_one) % n1 + (two - at_two) % n2 * n1
                    ordered.append(pick(part_rows, (mate - k) % mates * rows + index))
            return jnp.stack(ordered, 1).reshape(rows * depth, -1)

        def sum_first(panel, factor, inverse, *held):
            scaled = scale(factor, inverse)
            scaleds = [scaled]
            scaleds += [to_mate(scaled, step, f"scaled{panel}_swap") for step in range(1, mates)]
            each = n2 * piece
            sent = product(held, scaleds, each, (n1 - 1) * each, piece, jnp.bfloat16)
            sent = sent.reshape(n1 - 1, n2, piece, -1)
            received = [
                to_plane(sent[step - 1], 0, step, f"sum{panel}_first") for step in range(1, n1)
            ]
            half_sum = product(held, scaleds, 0, each, piece, jnp.float32).reshape(n2, piece, -1)
            for value in received:
                half_sum = half_sum + value
            return half_sum

        def sum_second(panel, half_sum):
            whole_sum = half_sum[0]
            for step in range(1, n2):
                part = half_sum[step].astype(jnp.bfloat16)
                whole_sum = whole_sum + to_plane(part, 1, step, f"sum{panel}_second")
            return whole_sum.astype(jnp.bfloat16)

        def ring(panel, own):
            return jnp.stack([own] + [to_plane(own, 0, a, f"ring{panel}_first") for a in range(1, n1)])

        def ring_rest(panel, pair):
            lefts = [pair] + [to_plane(pair, 1, b, f"ring{panel}_second") for b in range(1, n2)]
            return lefts + [
                to_mate(value, step, f"ring{panel}_swap")
                for step in range(1, mates)
                for value in lefts
            ]

        def to_columns(panel, gathered):
            came = []
            for ds, dy in steps:
                target = (sec + ds) % secs * lanes + (lane + dy) % lanes

                def route(s, r, y, k):
                    v, w = (s + ds) % secs, (y + dy) % lanes
                    return (v, r, w, k) if r != v * lanes + w else None

                value = pick(gathered, target)
                came.append(send(value, route, f"column{panel}_{ds}{dy}"))
            return came

        places = []
        for step in range(mates):
            source = (mate - step) % mates
            one, two = first_second(source)
            for b in range(n2):
                for a in range(n1):
                    place = piece_of(source, (one - a) % n1, (two - b) % n2)
                    places.append(source * rows + place)
        places += [
            (sec - ds) % secs * lanes + (lane - dy) % lanes for ds, dy in [(0, 0)] + steps
        ]
        meta = jnp.stack([row - block, mate, *places, block]).astype(jnp.int32)
        always = (row + rows) // rows == 1

        def together(function, *values):
            shapes = jax.eval_shape(function, *values)
            zeros = lambda *_: jax.tree.map(lambda x: jnp.zeros(x.shape, x.dtype), shapes)
            return lax.cond(always, function, zeros, *values)

        part = depth // (mates * rows)
        group = block * mates + mate
        own_rows = lax.dynamic_slice_in_dim(block_inverses, group * part, part, 1)

        def prepare(own_rows, *shares):
            stack = lax.all_gather(own_rows, "row")
            held = [to_mate(value, step + 1, "held_swap") for step, value in enumerate(shares)]
            return [whole_inverse(stack[:, p], f"inverse{p}") for p in range(panels)], held

        shares = [share(step) for step in range(mates)]
        factors = {0: lax.all_gather(factor_panels[0], "row")}
        inverses, swapped = together(prepare, own_rows, *shares[1:])
        held = [shares[0]] + swapped

        total, owns, moved, lefts = covariance, {}, {}, {}
        for now in range(panels + 2):
            state = fence(factors, inverses, held, total, owns, moved, lefts)
            factors, inverses, held, total, owns, moved, lefts = state
            if now + 1 < panels:
                ahead, factors[now] = fence(factor_panels[now + 1], factors[now])
                factors[now + 1] = lax.all_gather(ahead, "row")
            if 0 <= now - 1 < panels:
                moved[now - 1] = lax.all_gather(owns[now - 1], "row")

            def work(factor, held, inverse, own, total, lefts, moved):
                following = None
                if own is not None:
                    pair = ring(now - 1, own)
                if factor is not None:
                    following = sum_first(now, factor, inverse, *held)
                if lefts is not None:
                    came = to_columns(now - 2, moved)
                    if own is not None:
                        pair, came = fence(pair, came)
                if own is not None:
                    own = ring_rest(now - 1, pair)
                if factor is not None:
                    following = sum_second(now, following)
                if lefts is not None:
                    total = update(meta, total, lefts, moved, came)
                return following, own, total if lefts is not None else None

            operands = (
                factors.get(now),
                held if now < panels else None,
                inverses[now] if now < panels else None,
                owns.get(now - 1),
                total if now >= 2 else None,
                lefts.get(now - 2),
                moved.get(now - 2),
            )
            step = together if now < panels + 1 else lambda function, *values: function(*values)
            following, around, latest = step(work, *operands)
            if following is not None:
                owns[now] = following
            if around is not None:
                lefts[now - 1] = around
            if latest is not None:
                total = latest
        return total

    return body


def solution(mesh):
    in_specs = (
        P("row", ("sec", "col")),
        P(None, ("sec", "col"), "row"),
        P(None, "row", None),
        P("row", ("sec", "col")),
    )
    out_specs = P("row", ("sec", "col"))
    return jax.shard_map(
        make_body(dict(mesh.shape)), mesh=mesh, in_specs=in_specs, out_specs=out_specs, check_vma=False
    )
```

```python
import jax
import jax.numpy as jnp
from jax import lax
from jax.experimental import pallas as pl
from jax.experimental.pallas import tpu as pltpu
from jax.sharding import PartitionSpec as P

AXES = ("sec", "row", "col")
HALVES = 2


def pick(array, index):
    return lax.dynamic_index_in_dim(array, index, 0, keepdims=False)


def make_body(shape):
    secs, rows, cols = (shape[axis] for axis in AXES)
    mates = secs * cols // rows
    lanes = cols // mates
    swaps = secs == lanes
    sizes = (secs, lanes)
    steps = [(ds, dy) for dy in range(lanes) for ds in range(secs) if ds or dy]

    def send(value, route, name):
        pairs = []
        for s in range(secs):
            for r in range(rows):
                for y in range(lanes):
                    for k in range(mates):
                        to = route(s, r, y, k)
                        if to is not None:
                            t, q, v, m = to
                            source = (s * rows + r) * cols + y * mates + k
                            pairs.append((source, (t * rows + q) * cols + v * mates + m))
        with jax.named_scope(name):
            return lax.ppermute(value, AXES, pairs)

    def to_mate(value, step, name):
        return send(value, lambda s, r, y, k: (s, r, y, (k + step) % mates), name)

    def to_plane(value, phase, step, name):
        def route(s, r, y, k):
            along_sec = phase == (1 if swaps and k % 2 else 0)
            if along_sec:
                return ((s + step) % secs, r, y, k)
            return (s, r, (y + step) % lanes, k)

        return send(value, route, name)

    params = pltpu.CompilerParams(vmem_limit_bytes=40 * 2**20)

    def reorder(order, array):
        _, planes, height, width = array.shape
        count = order.shape[0]

        def kernel(order_ref, in_ref, out_ref):
            for plane in range(planes):
                out_ref[plane, 0] = in_ref[0, plane]

        return pl.pallas_call(
            kernel,
            out_shape=jax.ShapeDtypeStruct((planes, count, height, width), array.dtype),
            grid_spec=pltpu.PrefetchScalarGridSpec(
                num_scalar_prefetch=1,
                grid=(count,),
                in_specs=[
                    pl.BlockSpec((1, planes, height, width), lambda i, order_ref: (order_ref[i], 0, 0, 0))
                ],
                out_specs=pl.BlockSpec((planes, 1, height, width), lambda i, order_ref: (0, i, 0, 0)),
            ),
            compiler_params=params,
            cost_estimate=pl.CostEstimate(
                flops=0, bytes_accessed=4 * count * planes * height * width, transcendentals=0
            ),
        )(order, array)

    def scale(factor, inverse):
        _, tile, depth = factor.shape
        full, width = inverse.shape
        chunk = tile // rows

        def kernel(factor_ref, inverse_ref, out_ref):
            out_ref[...] = jnp.dot(
                jnp.concatenate([factor_ref[i] for i in range(rows)], 1),
                inverse_ref[...],
                preferred_element_type=jnp.float32,
            ).astype(out_ref.dtype)

        return pl.pallas_call(
            kernel,
            out_shape=jax.ShapeDtypeStruct((tile, width), factor.dtype),
            grid=(tile // chunk,),
            in_specs=[
                pl.BlockSpec((rows, chunk, depth), lambda i: (0, i, 0)),
                pl.BlockSpec((full, width), lambda i: (0, 0)),
            ],
            out_specs=pl.BlockSpec((chunk, width), lambda i: (i, 0)),
            compiler_params=params,
            cost_estimate=pl.CostEstimate(
                flops=2 * tile * full * width,
                bytes_accessed=2 * (tile * full + full * width + tile * width),
                transcendentals=0,
            ),
        )(factor, inverse)

    def product(held, scaleds, first, count, piece, kind):
        tile, width = scaleds[0].shape

        def kernel(*refs):
            left, right, out_ref = refs[:mates], refs[mates:-1], refs[-1]
            total = jnp.dot(left[0][...], right[0][...], preferred_element_type=jnp.float32)
            for step in range(1, mates):
                total += jnp.dot(
                    left[step][...], right[step][...], preferred_element_type=jnp.float32
                )
            out_ref[...] = total.astype(out_ref.dtype)

        offset = first // piece
        return pl.pallas_call(
            kernel,
            out_shape=jax.ShapeDtypeStruct((count, width), kind),
            grid=(count // piece,),
            in_specs=[pl.BlockSpec((piece, tile), lambda i: (i + offset, 0))] * mates
            + [pl.BlockSpec((tile, width), lambda i: (0, 0))] * mates,
            out_specs=pl.BlockSpec((piece, width), lambda i: (i, 0)),
            compiler_params=params,
            cost_estimate=pl.CostEstimate(
                flops=2 * mates * count * tile * width,
                bytes_accessed=2 * mates * tile * (count + width) + 4 * count * width,
                transcendentals=0,
            ),
        )(*held, *scaleds)

    def update(meta, total, lefts, rights):
        n1, piece, width = lefts[0].shape
        height, tile = total.shape
        n_left, sub = len(lefts) * n1, piece // HALVES
        span = tile // HALVES
        halves = list(rights)
        sources = [[gathered, *came] for gathered, _, came in rights.values()]
        operands = [*lefts, *[value for group in sources for value in group]]

        def kernel(meta_ref, total_ref, *refs):
            left, out_ref, left_buf, right_buf, left_sem, right_sem = refs[: len(lefts)], *refs[-5:]
            gap, mate, own = meta_ref[0], meta_ref[1], meta_ref[2]
            base = 3

            def left_copy(i, h):
                source = left[i // n1].at[i % n1, pl.ds(h * sub, sub)]
                start = meta_ref[base + i] + h * span
                to = pl.ds(pl.multiple_of(start, sub), sub)
                return pltpu.make_async_copy(source, left_buf.at[to], left_sem.at[start // sub])

            def right_copy(j, at, source, place):
                to = pl.ds(pl.multiple_of(place + at * span, sub), sub)
                return pltpu.make_async_copy(source, right_buf.at[to], right_sem.at[j, at])

            @pl.when(pl.program_id(0) == 0)
            def _():
                for at, h in enumerate(halves):
                    gathered, *came = refs[len(lefts) + at * rows :][:rows]
                    lines = pl.ds(rights[h][1], sub)
                    for j in range(rows):

                        @pl.when(gap == 0)
                        def _():
                            source = left[j // n1].at[j % n1, pl.ds(h * sub, sub)]
                            right_copy(j, at, source, meta_ref[base + j] - mate * tile).start()

                        @pl.when(gap != 0)
                        def _():
                            source = came[j - 1].at[lines] if j else gathered.at[own, lines]
                            right_copy(j, at, source, meta_ref[base + n_left + j]).start()

                for i in range(n_left):
                    for h in range(HALVES):
                        left_copy(i, h).start()
                for at in range(len(halves)):
                    for j in range(rows):
                        right_copy(j, at, left[0].at[0, pl.ds(0, sub)], 0).wait()

            for h in range(HALVES):
                at = pl.program_id(0) * HALVES + h
                pltpu.make_async_copy(
                    left[0].at[0, pl.ds(0, sub)], left_buf.at[pl.ds(0, sub)], left_sem.at[at]
                ).wait()
            lines = pl.ds(pl.multiple_of(pl.program_id(0) * piece, piece), piece)
            out_ref[...] = total_ref[...] + lax.dot_general(
                left_buf[lines],
                right_buf[...],
                (((1,), (1,)), ((), ())),
                preferred_element_type=jnp.float32,
            )

        first = halves[0]
        columns = span * len(halves)
        block = pl.BlockSpec((piece, columns), lambda i, meta_ref: (i, first))
        return pl.pallas_call(
            kernel,
            out_shape=jax.ShapeDtypeStruct(total.shape, total.dtype),
            grid_spec=pltpu.PrefetchScalarGridSpec(
                num_scalar_prefetch=1,
                grid=(n_left,),
                in_specs=[block] + [pl.BlockSpec(memory_space=pl.ANY)] * len(operands),
                out_specs=block,
                scratch_shapes=[
                    pltpu.VMEM((height, width), jnp.bfloat16),
                    pltpu.VMEM((columns, width), jnp.bfloat16),
                    pltpu.SemaphoreType.DMA((n_left * HALVES,)),
                    pltpu.SemaphoreType.DMA((rows, len(halves))),
                ],
            ),
            input_output_aliases={} if len(halves) == HALVES else {1: 0},
            compiler_params=params,
            cost_estimate=pl.CostEstimate(
                flops=2 * height * columns * width,
                bytes_accessed=8 * height * columns + 2 * width * (height + columns),
                transcendentals=0,
            ),
        )(meta, total, *operands)

    def body(held_inverse, factor_panels, block_inverses, covariance):
        panels, tile, depth = factor_panels.shape
        sec, row = lax.axis_index("sec"), lax.axis_index("row")
        lane, mate = lax.axis_index("col") // mates, lax.axis_index("col") % mates
        block = sec * lanes + lane
        piece = tile // (secs * lanes)
        n1, n2 = sizes

        def first_second(mate):
            if not swaps:
                return sec, lane
            odd = mate % 2 == 1
            return jnp.where(odd, lane, sec), jnp.where(odd, sec, lane)

        def piece_of(mate, one, two):
            if not swaps:
                return one * lanes + two
            return jnp.where(mate % 2 == 1, two * lanes + one, one * lanes + two)

        def fence(*values):
            return lax.optimization_barrier(values)

        sub = piece // HALVES
        blocks = held_inverse.reshape(mates * HALVES * rows, 1, sub, tile)

        def share(blocks, step):
            target = (mate + step) % mates
            one, two = first_second(target)
            order = [
                (target * HALVES + h) * rows + piece_of(target, (one + a) % n1, (two + b) % n2)
                for a in range(n1)
                for b in range(n2)
                for h in range(HALVES)
            ]
            return reorder(jnp.stack(order).astype(jnp.int32), blocks).reshape(tile, tile)

        def whole_inverse(stack, name):
            part_rows = stack[None]
            for phase, size in enumerate(sizes):
                kept = part_rows
                for step in range(1, size):
                    moved = to_plane(kept, phase, step, f"{name}_plane{phase}")
                    part_rows = jnp.concatenate([part_rows, moved])
            kept = part_rows
            for step in range(1, mates):
                part_rows = jnp.concatenate([part_rows, to_mate(kept, step, f"{name}_swap")])
            ordered = []
            for q in range(rows):
                for k in range(mates):
                    one, two = first_second(k)
                    at_one, at_two = q // lanes, q % lanes
                    if swaps and k % 2:
                        at_one, at_two = at_two, at_one
                    index = (one - at_one) % n1 + (two - at_two) % n2 * n1
                    ordered.append((mate - k) % mates * rows + index)
            order = jnp.stack(ordered).astype(jnp.int32)
            return reorder(order, part_rows).reshape(rows * depth, -1)

        def sum_first(panel, factor, inverse, around, *held):
            scaled = scale(factor, inverse)
            scaleds = [scaled]
            scaleds += [to_mate(scaled, step, f"scaled{panel}_swap") for step in range(1, mates)]
            each = n2 * piece
            sent = product(held, scaleds, each, (n1 - 1) * each, piece, jnp.bfloat16)
            sent, around = fence(sent.reshape(n1 - 1, n2, piece, -1), around)
            received = [
                to_plane(sent[step - 1], 0, step, f"sum{panel}_first") for step in range(1, n1)
            ]
            half_sum = product(held, scaleds, 0, each, piece, jnp.float32).reshape(n2, piece, -1)
            for value in received:
                half_sum = half_sum + value
            return half_sum, around

        def sum_second(panel, half_sum):
            whole_sum = half_sum[0]
            for step in range(1, n2):
                part = half_sum[step].astype(jnp.bfloat16)
                whole_sum = whole_sum + to_plane(part, 1, step, f"sum{panel}_second")
            return whole_sum.astype(jnp.bfloat16)

        def halved(own):
            return [own[h * sub : (h + 1) * sub] for h in range(HALVES)]

        def ring(panel, own):
            return jnp.stack([own] + [to_plane(own, 0, a, f"ring{panel}_first") for a in range(1, n1)])

        def ring_rest(panel, pair):
            return [pair] + [to_plane(pair, 1, b, f"ring{panel}_second") for b in range(1, n2)]

        def ring_swap(panel, lefts):
            return lefts + [
                to_mate(value, step, f"ring{panel}_swap")
                for step in range(1, mates)
                for value in lefts
            ]

        def to_columns(name, gathered):
            came = []
            for ds, dy in steps:
                target = (sec + ds) % secs * lanes + (lane + dy) % lanes

                def route(s, r, y, k):
                    return ((s + ds) % secs, r, (y + dy) % lanes, k)

                value = pick(gathered, target)
                came.append(send(value, route, f"column{name}_{ds}{dy}"))
            return came

        places = []
        for step in range(mates):
            source = (mate - step) % mates
            one, two = first_second(source)
            for b in range(n2):
                for a in range(n1):
                    place = piece_of(source, (one - a) % n1, (two - b) % n2)
                    places.append(source * tile + place * sub)
        places += [
            ((sec - ds) % secs * lanes + (lane - dy) % lanes) * sub for ds, dy in [(0, 0)] + steps
        ]
        meta = jnp.stack([row - block, mate, block, *places]).astype(jnp.int32)
        always = (row + rows) // rows == 1

        def together(function, *values):
            shapes = jax.eval_shape(function, *values)
            zeros = lambda *_: jax.tree.map(lambda x: jnp.zeros(x.shape, x.dtype), shapes)
            return lax.cond(always, function, zeros, *values)

        part = depth // (mates * rows)
        group = block * mates + mate
        own_rows = lax.dynamic_slice_in_dim(block_inverses, group * part, part, 1)

        def prepare(own_rows, blocks):
            stack, blocks = fence(lax.all_gather(own_rows, "row"), blocks)
            shares = [share(blocks, step) for step in range(mates)]
            held = [shares[0]] + [to_mate(shares[step], step, "held_swap") for step in range(1, mates)]
            return [whole_inverse(stack[:, p], f"inverse{p}") for p in range(panels)], held

        factors = {0: lax.all_gather(factor_panels[0], "row")}
        inverses, held = together(prepare, own_rows, blocks)

        def both(gathered, came):
            return {h: (gathered, h * sub, came) for h in range(HALVES)}

        total, owns, pairs, moved, lefts = covariance, {}, {}, {}, {}
        for now in range(panels):
            state = fence(factors, inverses, held, total, owns, pairs, moved, lefts)
            factors, inverses, held, total, owns, pairs, moved, lefts = state
            if now + 1 < panels:
                factor_panels, factors[now] = fence(factor_panels, factors[now])
                factors[now + 1] = lax.all_gather(factor_panels[now + 1], "row")
            if now >= 1:
                moved[now - 1] = lax.all_gather(owns[now - 1], "row")

            def work(factor, held, inverse, pair, total, lefts, moved):
                around = latest = None
                if pair is not None:
                    around = ring_rest(now - 1, pair)
                half_sum, around = sum_first(now, factor, inverse, around, *held)
                own = sum_second(now, half_sum)
                if lefts is not None:
                    latest = update(meta, total, lefts, both(moved, to_columns(now - 2, moved)))
                if pair is not None:
                    around = ring_swap(now - 1, around)
                if now + 1 < panels:
                    return own, ring(now, own), around, latest
                return own, halved(own), around, latest

            owns[now], pairs[now], around, latest = together(
                work,
                factors[now],
                held,
                inverses[now],
                pairs.get(now - 1),
                total if now >= 2 else None,
                lefts.get(now - 2),
                moved.get(now - 2),
            )
            if around is not None:
                lefts[now - 1] = around
            if latest is not None:
                total = latest

        own, parts, moved, lefts, total = fence(owns[panels - 1], pairs[panels - 1], moved, lefts, total)
        gathered = {0: lax.all_gather(parts[0], "row")}

        def first_work(own, value):
            came = to_columns(panels - 2, value) if value is not None else None
            return ring(panels - 1, own), came

        pair, came = together(first_work, own, moved.get(panels - 2))
        arrived = {}
        for h in range(HALVES):
            state = fence(parts, pair, moved, lefts, total, gathered, came, arrived)
            parts, pair, moved, lefts, total, gathered, came, arrived = state
            if h + 1 < HALVES:
                gathered[h + 1] = lax.all_gather(parts[h + 1], "row")
            if h == 0:

                def last_work(value, pair, total, lefts, moved, came):
                    steps_done = to_columns(f"{panels - 1}_half0", value)
                    around = ring_rest(panels - 1, pair)
                    if came is not None:
                        total = update(meta, total, lefts, both(moved, came))
                        around, total, steps_done = fence(around, total, steps_done)
                    return steps_done, ring_swap(panels - 1, around), total if came is not None else None

                arrived[0], around, latest = together(
                    last_work,
                    gathered[0],
                    pair,
                    total if panels > 1 else None,
                    lefts.get(panels - 2),
                    moved.get(panels - 2),
                    came,
                )
                if latest is not None:
                    total = latest
            else:
                arrived[h] = to_columns(f"{panels - 1}_half{h}", gathered[h])
                total = update(meta, total, around, {h - 1: (gathered[h - 1], 0, arrived[h - 1])})
        total = update(meta, total, around, {HALVES - 1: (gathered[HALVES - 1], 0, arrived[HALVES - 1])})
        return total

    return body


def solution(mesh):
    in_specs = (
        P("row", ("sec", "col")),
        P(None, ("sec", "col"), "row"),
        P(None, "row", None),
        P("row", ("sec", "col")),
    )
    out_specs = P("row", ("sec", "col"))
    return jax.shard_map(
        make_body(dict(mesh.shape)), mesh=mesh, in_specs=in_specs, out_specs=out_specs, check_vma=False
    )
```

```python
import jax
import jax.numpy as jnp
from jax import lax
from jax.experimental import pallas as pl
from jax.experimental.pallas import tpu as pltpu
from jax.sharding import PartitionSpec as P

AXES = ("sec", "row", "col")
HALVES = 2


def pick(array, index):
    return lax.dynamic_index_in_dim(array, index, 0, keepdims=False)


def make_body(shape):
    secs, rows, cols = (shape[axis] for axis in AXES)
    mates = secs * cols // rows
    lanes = cols // mates
    swaps = secs == lanes
    sizes = (secs, lanes)
    steps = [(ds, dy) for dy in range(lanes) for ds in range(secs) if ds or dy]

    def send(value, route, name):
        pairs = []
        for s in range(secs):
            for r in range(rows):
                for y in range(lanes):
                    for k in range(mates):
                        to = route(s, r, y, k)
                        if to is not None:
                            t, q, v, m = to
                            source = (s * rows + r) * cols + y * mates + k
                            pairs.append((source, (t * rows + q) * cols + v * mates + m))
        with jax.named_scope(name):
            return lax.ppermute(value, AXES, pairs)

    def to_mate(value, step, name):
        return send(value, lambda s, r, y, k: (s, r, y, (k + step) % mates), name)

    def to_plane(value, phase, step, name):
        def route(s, r, y, k):
            along_sec = phase == (1 if swaps and k % 2 else 0)
            if along_sec:
                return ((s + step) % secs, r, y, k)
            return (s, r, (y + step) % lanes, k)

        return send(value, route, name)

    params = pltpu.CompilerParams(vmem_limit_bytes=40 * 2**20)

    def reorder(order, array):
        _, planes, height, width = array.shape
        count = order.shape[0]

        def kernel(order_ref, in_ref, out_ref):
            for plane in range(planes):
                out_ref[plane, 0] = in_ref[0, plane]

        return pl.pallas_call(
            kernel,
            out_shape=jax.ShapeDtypeStruct((planes, count, height, width), array.dtype),
            grid_spec=pltpu.PrefetchScalarGridSpec(
                num_scalar_prefetch=1,
                grid=(count,),
                in_specs=[
                    pl.BlockSpec((1, planes, height, width), lambda i, order_ref: (order_ref[i], 0, 0, 0))
                ],
                out_specs=pl.BlockSpec((planes, 1, height, width), lambda i, order_ref: (0, i, 0, 0)),
            ),
            compiler_params=params,
            cost_estimate=pl.CostEstimate(
                flops=0, bytes_accessed=4 * count * planes * height * width, transcendentals=0
            ),
        )(order, array)

    def scale(factor, inverse):
        _, tile, depth = factor.shape
        full, width = inverse.shape
        chunk = tile // rows

        def kernel(factor_ref, inverse_ref, out_ref):
            out_ref[...] = jnp.dot(
                jnp.concatenate([factor_ref[i] for i in range(rows)], 1),
                inverse_ref[...],
                preferred_element_type=jnp.float32,
            ).astype(out_ref.dtype)

        return pl.pallas_call(
            kernel,
            out_shape=jax.ShapeDtypeStruct((tile, width), factor.dtype),
            grid=(tile // chunk,),
            in_specs=[
                pl.BlockSpec((rows, chunk, depth), lambda i: (0, i, 0)),
                pl.BlockSpec((full, width), lambda i: (0, 0)),
            ],
            out_specs=pl.BlockSpec((chunk, width), lambda i: (i, 0)),
            compiler_params=params,
            cost_estimate=pl.CostEstimate(
                flops=2 * tile * full * width,
                bytes_accessed=2 * (tile * full + full * width + tile * width),
                transcendentals=0,
            ),
        )(factor, inverse)

    def product(held, scaleds, first, count, piece, kind):
        tile, width = scaleds[0].shape

        def kernel(*refs):
            left, right, out_ref = refs[:mates], refs[mates:-1], refs[-1]
            total = jnp.dot(left[0][...], right[0][...], preferred_element_type=jnp.float32)
            for step in range(1, mates):
                total += jnp.dot(
                    left[step][...], right[step][...], preferred_element_type=jnp.float32
                )
            out_ref[...] = total.astype(out_ref.dtype)

        offset = first // piece
        return pl.pallas_call(
            kernel,
            out_shape=jax.ShapeDtypeStruct((count, width), kind),
            grid=(count // piece,),
            in_specs=[pl.BlockSpec((piece, tile), lambda i: (i + offset, 0))] * mates
            + [pl.BlockSpec((tile, width), lambda i: (0, 0))] * mates,
            out_specs=pl.BlockSpec((piece, width), lambda i: (i, 0)),
            compiler_params=params,
            cost_estimate=pl.CostEstimate(
                flops=0, bytes_accessed=0, transcendentals=0
            ),
        )(*held, *scaleds)

    def update(meta, total, lefts, rights):
        n1, piece, width = lefts[0].shape
        height, tile = total.shape
        n_left, sub = len(lefts) * n1, piece // HALVES
        span = tile // HALVES
        halves = list(rights)
        sources = [[gathered, *came] for gathered, _, came in rights.values()]
        operands = [*lefts, *[value for group in sources for value in group]]

        def kernel(meta_ref, total_ref, *refs):
            left, out_ref, left_buf, right_buf, left_sem, right_sem = refs[: len(lefts)], *refs[-5:]
            gap, mate, own = meta_ref[0], meta_ref[1], meta_ref[2]
            base = 3

            def left_copy(i, h):
                source = left[i // n1].at[i % n1, pl.ds(h * sub, sub)]
                start = meta_ref[base + i] + h * span
                to = pl.ds(pl.multiple_of(start, sub), sub)
                return pltpu.make_async_copy(source, left_buf.at[to], left_sem.at[start // sub])

            def right_copy(j, at, source, place):
                to = pl.ds(pl.multiple_of(place + at * span, sub), sub)
                return pltpu.make_async_copy(source, right_buf.at[to], right_sem.at[j, at])

            @pl.when(pl.program_id(0) == 0)
            def _():
                for at, h in enumerate(halves):
                    gathered, *came = refs[len(lefts) + at * rows :][:rows]
                    lines = pl.ds(rights[h][1], sub)
                    for j in range(rows):

                        @pl.when(gap == 0)
                        def _():
                            source = left[j // n1].at[j % n1, pl.ds(h * sub, sub)]
                            right_copy(j, at, source, meta_ref[base + j] - mate * tile).start()

                        @pl.when(gap != 0)
                        def _():
                            source = came[j - 1].at[lines] if j else gathered.at[own, lines]
                            right_copy(j, at, source, meta_ref[base + n_left + j]).start()

                for i in range(n_left):
                    for h in range(HALVES):
                        left_copy(i, h).start()
                for at in range(len(halves)):
                    for j in range(rows):
                        right_copy(j, at, left[0].at[0, pl.ds(0, sub)], 0).wait()

            for h in range(HALVES):
                at = pl.program_id(0) * HALVES + h
                pltpu.make_async_copy(
                    left[0].at[0, pl.ds(0, sub)], left_buf.at[pl.ds(0, sub)], left_sem.at[at]
                ).wait()
            lines = pl.ds(pl.multiple_of(pl.program_id(0) * piece, piece), piece)
            out_ref[...] = total_ref[...] + lax.dot_general(
                left_buf[lines],
                right_buf[...],
                (((1,), (1,)), ((), ())),
                preferred_element_type=jnp.float32,
            )

        first = halves[0]
        columns = span * len(halves)
        block = pl.BlockSpec((piece, columns), lambda i, meta_ref: (i, first))
        return pl.pallas_call(
            kernel,
            out_shape=jax.ShapeDtypeStruct(total.shape, total.dtype),
            grid_spec=pltpu.PrefetchScalarGridSpec(
                num_scalar_prefetch=1,
                grid=(n_left,),
                in_specs=[block] + [pl.BlockSpec(memory_space=pl.ANY)] * len(operands),
                out_specs=block,
                scratch_shapes=[
                    pltpu.VMEM((height, width), jnp.bfloat16),
                    pltpu.VMEM((columns, width), jnp.bfloat16),
                    pltpu.SemaphoreType.DMA((n_left * HALVES,)),
                    pltpu.SemaphoreType.DMA((rows, len(halves))),
                ],
            ),
            input_output_aliases={} if len(halves) == HALVES else {1: 0},
            compiler_params=params,
            cost_estimate=pl.CostEstimate(
                flops=2 * height * columns * width,
                bytes_accessed=8 * height * columns + 2 * width * (height + columns),
                transcendentals=0,
            ),
        )(meta, total, *operands)

    def body(held_inverse, factor_panels, block_inverses, covariance):
        panels, tile, depth = factor_panels.shape
        sec, row = lax.axis_index("sec"), lax.axis_index("row")
        lane, mate = lax.axis_index("col") // mates, lax.axis_index("col") % mates
        block = sec * lanes + lane
        piece = tile // (secs * lanes)
        n1, n2 = sizes

        def first_second(mate):
            if not swaps:
                return sec, lane
            odd = mate % 2 == 1
            return jnp.where(odd, lane, sec), jnp.where(odd, sec, lane)

        def piece_of(mate, one, two):
            if not swaps:
                return one * lanes + two
            return jnp.where(mate % 2 == 1, two * lanes + one, one * lanes + two)

        def fence(*values):
            return lax.optimization_barrier(values)

        sub = piece // HALVES
        blocks = held_inverse.reshape(mates * HALVES * rows, 1, sub, tile)

        def share(blocks, step):
            target = (mate + step) % mates
            one, two = first_second(target)
            order = [
                (target * HALVES + h) * rows + piece_of(target, (one + a) % n1, (two + b) % n2)
                for a in range(n1)
                for b in range(n2)
                for h in range(HALVES)
            ]
            return reorder(jnp.stack(order).astype(jnp.int32), blocks).reshape(tile, tile)

        def whole_inverse(stack, name):
            part_rows = stack[None]
            for phase, size in enumerate(sizes):
                kept = part_rows
                for step in range(1, size):
                    moved = to_plane(kept, phase, step, f"{name}_plane{phase}")
                    part_rows = jnp.concatenate([part_rows, moved])
            kept = part_rows
            for step in range(1, mates):
                part_rows = jnp.concatenate([part_rows, to_mate(kept, step, f"{name}_swap")])
            ordered = []
            for q in range(rows):
                for k in range(mates):
                    one, two = first_second(k)
                    at_one, at_two = q // lanes, q % lanes
                    if swaps and k % 2:
                        at_one, at_two = at_two, at_one
                    index = (one - at_one) % n1 + (two - at_two) % n2 * n1
                    ordered.append((mate - k) % mates * rows + index)
            order = jnp.stack(ordered).astype(jnp.int32)
            return reorder(order, part_rows).reshape(rows * depth, -1)

        def sum_first(panel, factor, inverse, *held):
            scaled = scale(factor, inverse)
            scaleds = [scaled]
            scaleds += [to_mate(scaled, step, f"scaled{panel}_swap") for step in range(1, mates)]
            each = n2 * piece
            sent = product(held, scaleds, each, (n1 - 1) * each, piece, jnp.bfloat16)
            sent = sent.reshape(n1 - 1, n2, piece, -1)
            received = [
                to_plane(sent[step - 1], 0, step, f"sum{panel}_first") for step in range(1, n1)
            ]
            half_sum = product(held, scaleds, 0, each, piece, jnp.float32).reshape(n2, piece, -1)
            for value in received:
                half_sum = half_sum + value
            return half_sum

        def sum_second(panel, half_sum):
            whole_sum = half_sum[0]
            for step in range(1, n2):
                part = half_sum[step].astype(jnp.bfloat16)
                whole_sum = whole_sum + to_plane(part, 1, step, f"sum{panel}_second")
            return whole_sum.astype(jnp.bfloat16)

        def halved(own):
            return [own[h * sub : (h + 1) * sub] for h in range(HALVES)]

        def ring(panel, own):
            return jnp.stack([own] + [to_plane(own, 0, a, f"ring{panel}_first") for a in range(1, n1)])

        def ring_rest(panel, pair):
            return [pair] + [to_plane(pair, 1, b, f"ring{panel}_second") for b in range(1, n2)]

        def ring_swap(panel, lefts):
            return [
                [to_mate(value, step, f"ring{panel}_swap") for value in lefts]
                for step in range(1, mates)
            ]

        def joined(lefts, swapped):
            return sum(swapped, lefts)

        def to_columns(name, gathered):
            came = []
            for ds, dy in steps:
                target = (sec + ds) % secs * lanes + (lane + dy) % lanes

                def route(s, r, y, k):
                    return ((s + ds) % secs, r, (y + dy) % lanes, k)

                value = pick(gathered, target)
                came.append(send(value, route, f"column{name}_{ds}{dy}"))
            return came

        places = []
        for step in range(mates):
            source = (mate - step) % mates
            one, two = first_second(source)
            for b in range(n2):
                for a in range(n1):
                    place = piece_of(source, (one - a) % n1, (two - b) % n2)
                    places.append(source * tile + place * sub)
        places += [
            ((sec - ds) % secs * lanes + (lane - dy) % lanes) * sub for ds, dy in [(0, 0)] + steps
        ]
        meta = jnp.stack([row - block, mate, block, *places]).astype(jnp.int32)
        always = (row + rows) // rows == 1

        def together(function, *values):
            shapes = jax.eval_shape(function, *values)
            zeros = lambda *_: jax.tree.map(lambda x: jnp.zeros(x.shape, x.dtype), shapes)
            return lax.cond(always, function, zeros, *values)

        part = depth // (mates * rows)
        group = block * mates + mate
        own_rows = lax.dynamic_slice_in_dim(block_inverses, group * part, part, 1)

        def prepare(own_rows, blocks, factor_panels):
            stack, blocks = fence(lax.all_gather(own_rows, "row"), blocks)
            shares = [share(blocks, step) for step in range(mates)]
            held = [shares[0]] + [to_mate(shares[step], step, "held_swap") for step in range(1, mates)]
            inverses = [whole_inverse(stack[:, p], f"inverse{p}") for p in range(panels)]
            return inverses, held, [factor_panels[p] for p in range(1, panels)]

        factors = {0: lax.all_gather(factor_panels[0], "row")}
        inverses, held, waiting = together(prepare, own_rows, blocks, factor_panels)

        def both(gathered, came):
            return {h: (gathered, h * sub, came) for h in range(HALVES)}

        total, owns, pairs, moved, rests = covariance, {}, {}, {}, {}
        for now in range(panels):
            state = fence(factors, inverses, held, total, owns, pairs, moved, rests)
            factors, inverses, held, total, owns, pairs, moved, rests = state
            if now + 1 < panels:
                waiting, factors[now] = fence(waiting, factors[now])
                factors[now + 1] = lax.all_gather(waiting[now], "row")
            if now >= 1:
                moved[now - 1] = lax.all_gather(owns[now - 1], "row")
                rests[now - 1] = ring_rest(now - 1, pairs[now - 1])

            def work(factor, held, inverse, total, rest, moved):
                own = sum_second(now, sum_first(now, factor, inverse, *held))
                latest = None
                if rest is not None:
                    lefts, came = joined(rest, ring_swap(now - 2, rest)), to_columns(now - 2, moved)
                    latest = update(meta, total, lefts, both(moved, came))
                return own, halved(own), ring(now, own), latest

            owns[now], parts, pairs[now], latest = together(
                work,
                factors[now],
                held,
                inverses[now],
                total if now >= 2 else None,
                rests.get(now - 2),
                moved.get(now - 2),
            )
            if latest is not None:
                total = latest

        parts, pair, moved, rests, total = fence(parts, pairs[panels - 1], moved, rests, total)
        gathered = {0: lax.all_gather(parts[0], "row")}

        def first_work(value, rest, pair):
            came = swapped = None
            if value is not None:
                came, swapped = to_columns(panels - 2, value), ring_swap(panels - 2, rest)
            return came, swapped, ring_swap(panels - 1, [pair])

        came, swapped, near = together(first_work, moved.get(panels - 2), rests.get(panels - 2), pair)
        lefts = {}
        if panels > 1:
            lefts[panels - 2] = joined(rests[panels - 2], swapped)
        arrived = {}
        for h in range(HALVES):
            state = fence(parts, pair, near, moved, lefts, total, gathered, came, arrived)
            parts, pair, near, moved, lefts, total, gathered, came, arrived = state
            if h + 1 < HALVES:
                gathered[h + 1] = lax.all_gather(parts[h + 1], "row")
            if h == 0:

                def last_work(value, pair, total, lefts, moved, came):
                    steps_done = to_columns(f"{panels - 1}_half0", value)
                    around = ring_rest(panels - 1, pair)
                    if came is not None:
                        total = update(meta, total, lefts, both(moved, came))
                        around, total, steps_done = fence(around, total, steps_done)
                    far = ring_swap(panels - 1, around[1:])
                    return steps_done, around[1:], far, total if came is not None else None

                arrived[0], rest, far, latest = together(
                    last_work,
                    gathered[0],
                    pair,
                    total if panels > 1 else None,
                    lefts.get(panels - 2),
                    moved.get(panels - 2),
                    came,
                )
                around = joined([pair, *rest], [one + two for one, two in zip(near, far)])
                if latest is not None:
                    total = latest
            else:
                arrived[h] = to_columns(f"{panels - 1}_half{h}", gathered[h])
                total = update(meta, total, around, {h - 1: (gathered[h - 1], 0, arrived[h - 1])})
        total = update(meta, total, around, {HALVES - 1: (gathered[HALVES - 1], 0, arrived[HALVES - 1])})
        return total

    return body


def solution(mesh):
    in_specs = (
        P("row", ("sec", "col")),
        P(None, ("sec", "col"), "row"),
        P(None, "row", None),
        P("row", ("sec", "col")),
    )
    out_specs = P("row", ("sec", "col"))
    return jax.shard_map(
        make_body(dict(mesh.shape)), mesh=mesh, in_specs=in_specs, out_specs=out_specs, check_vma=False
    )
```

```python
import jax
import jax.numpy as jnp
from jax import lax
from jax.experimental import pallas as pl
from jax.experimental.pallas import tpu as pltpu
from jax.sharding import PartitionSpec as P

AXES = ("sec", "row", "col")
HALVES = 2


def pick(array, index):
    return lax.dynamic_index_in_dim(array, index, 0, keepdims=False)


def make_body(shape):
    secs, rows, cols = (shape[axis] for axis in AXES)
    mates = secs * cols // rows
    lanes = cols // mates
    swaps = secs == lanes
    sizes = (secs, lanes)
    steps = [(ds, dy) for dy in range(lanes) for ds in range(secs) if ds or dy]

    def send(value, route, name):
        pairs = []
        for s in range(secs):
            for r in range(rows):
                for y in range(lanes):
                    for k in range(mates):
                        to = route(s, r, y, k)
                        if to is not None:
                            t, q, v, m = to
                            source = (s * rows + r) * cols + y * mates + k
                            pairs.append((source, (t * rows + q) * cols + v * mates + m))
        with jax.named_scope(name):
            return lax.ppermute(value, AXES, pairs)

    def to_mate(value, step, name):
        return send(value, lambda s, r, y, k: (s, r, y, (k + step) % mates), name)

    def to_plane(value, phase, step, name):
        def route(s, r, y, k):
            along_sec = phase == (1 if swaps and k % 2 else 0)
            if along_sec:
                return ((s + step) % secs, r, y, k)
            return (s, r, (y + step) % lanes, k)

        return send(value, route, name)

    params = pltpu.CompilerParams(vmem_limit_bytes=40 * 2**20)

    def reorder(order, array):
        _, planes, height, width = array.shape
        count = order.shape[0]

        def kernel(order_ref, in_ref, out_ref):
            for plane in range(planes):
                out_ref[plane, 0] = in_ref[0, plane]

        return pl.pallas_call(
            kernel,
            out_shape=jax.ShapeDtypeStruct((planes, count, height, width), array.dtype),
            grid_spec=pltpu.PrefetchScalarGridSpec(
                num_scalar_prefetch=1,
                grid=(count,),
                in_specs=[
                    pl.BlockSpec((1, planes, height, width), lambda i, order_ref: (order_ref[i], 0, 0, 0))
                ],
                out_specs=pl.BlockSpec((planes, 1, height, width), lambda i, order_ref: (0, i, 0, 0)),
            ),
            compiler_params=params,
            cost_estimate=pl.CostEstimate(
                flops=0, bytes_accessed=4 * count * planes * height * width, transcendentals=0
            ),
        )(order, array)

    def scale(factor, inverse):
        _, tile, depth = factor.shape
        full, width = inverse.shape
        chunk = tile // rows

        def kernel(factor_ref, inverse_ref, out_ref):
            out_ref[...] = jnp.dot(
                jnp.concatenate([factor_ref[i] for i in range(rows)], 1),
                inverse_ref[...],
                preferred_element_type=jnp.float32,
            ).astype(out_ref.dtype)

        return pl.pallas_call(
            kernel,
            out_shape=jax.ShapeDtypeStruct((tile, width), factor.dtype),
            grid=(tile // chunk,),
            in_specs=[
                pl.BlockSpec((rows, chunk, depth), lambda i: (0, i, 0)),
                pl.BlockSpec((full, width), lambda i: (0, 0)),
            ],
            out_specs=pl.BlockSpec((chunk, width), lambda i: (i, 0)),
            compiler_params=params,
            cost_estimate=pl.CostEstimate(
                flops=2 * tile * full * width,
                bytes_accessed=2 * (tile * full + full * width + tile * width),
                transcendentals=0,
            ),
        )(factor, inverse)

    def product(held, scaleds, first, count, piece, kind):
        tile, width = scaleds[0].shape

        def kernel(*refs):
            left, right, out_ref = refs[:mates], refs[mates:-1], refs[-1]
            total = jnp.dot(left[0][...], right[0][...], preferred_element_type=jnp.float32)
            for step in range(1, mates):
                total += jnp.dot(
                    left[step][...], right[step][...], preferred_element_type=jnp.float32
                )
            out_ref[...] = total.astype(out_ref.dtype)

        offset = first // piece
        return pl.pallas_call(
            kernel,
            out_shape=jax.ShapeDtypeStruct((count, width), kind),
            grid=(count // piece,),
            in_specs=[pl.BlockSpec((piece, tile), lambda i: (i + offset, 0))] * mates
            + [pl.BlockSpec((tile, width), lambda i: (0, 0))] * mates,
            out_specs=pl.BlockSpec((piece, width), lambda i: (i, 0)),
            compiler_params=params,
            cost_estimate=pl.CostEstimate(
                flops=0, bytes_accessed=0, transcendentals=0
            ),
        )(*held, *scaleds)

    def update(meta, total, lefts, rights):
        n1, piece, width = lefts[0].shape
        height, tile = total.shape
        n_left, sub = len(lefts) * n1, piece // HALVES
        span = tile // HALVES
        halves = list(rights)
        sources = [[gathered, *came] for gathered, _, came in rights.values()]
        operands = [*lefts, *[value for group in sources for value in group]]

        def kernel(meta_ref, total_ref, *refs):
            left, out_ref, left_buf, right_buf, left_sem, right_sem = refs[: len(lefts)], *refs[-5:]
            gap, mate, own = meta_ref[0], meta_ref[1], meta_ref[2]
            base = 3

            def left_copy(i, h):
                source = left[i // n1].at[i % n1, pl.ds(h * sub, sub)]
                start = meta_ref[base + i] + h * span
                to = pl.ds(pl.multiple_of(start, sub), sub)
                return pltpu.make_async_copy(source, left_buf.at[to], left_sem.at[start // sub])

            def right_copy(j, at, source, place):
                to = pl.ds(pl.multiple_of(place + at * span, sub), sub)
                return pltpu.make_async_copy(source, right_buf.at[to], right_sem.at[j, at])

            @pl.when(pl.program_id(0) == 0)
            def _():
                for at, h in enumerate(halves):
                    gathered, *came = refs[len(lefts) + at * rows :][:rows]
                    lines = pl.ds(rights[h][1], sub)
                    for j in range(rows):

                        @pl.when(gap == 0)
                        def _():
                            source = left[j // n1].at[j % n1, pl.ds(h * sub, sub)]
                            right_copy(j, at, source, meta_ref[base + j] - mate * tile).start()

                        @pl.when(gap != 0)
                        def _():
                            source = came[j - 1].at[lines] if j else gathered.at[own, lines]
                            right_copy(j, at, source, meta_ref[base + n_left + j]).start()

                for i in range(n_left):
                    for h in range(HALVES):
                        left_copy(i, h).start()
                for at in range(len(halves)):
                    for j in range(rows):
                        right_copy(j, at, left[0].at[0, pl.ds(0, sub)], 0).wait()

            for h in range(HALVES):
                at = pl.program_id(0) * HALVES + h
                pltpu.make_async_copy(
                    left[0].at[0, pl.ds(0, sub)], left_buf.at[pl.ds(0, sub)], left_sem.at[at]
                ).wait()
            lines = pl.ds(pl.multiple_of(pl.program_id(0) * piece, piece), piece)
            out_ref[...] = total_ref[...] + lax.dot_general(
                left_buf[lines],
                right_buf[...],
                (((1,), (1,)), ((), ())),
                preferred_element_type=jnp.float32,
            )

        first = halves[0]
        columns = span * len(halves)
        block = pl.BlockSpec((piece, columns), lambda i, meta_ref: (i, first))
        return pl.pallas_call(
            kernel,
            out_shape=jax.ShapeDtypeStruct(total.shape, total.dtype),
            grid_spec=pltpu.PrefetchScalarGridSpec(
                num_scalar_prefetch=1,
                grid=(n_left,),
                in_specs=[block] + [pl.BlockSpec(memory_space=pl.ANY)] * len(operands),
                out_specs=block,
                scratch_shapes=[
                    pltpu.VMEM((height, width), jnp.bfloat16),
                    pltpu.VMEM((columns, width), jnp.bfloat16),
                    pltpu.SemaphoreType.DMA((n_left * HALVES,)),
                    pltpu.SemaphoreType.DMA((rows, len(halves))),
                ],
            ),
            input_output_aliases={} if len(halves) == HALVES else {1: 0},
            compiler_params=params,
            cost_estimate=pl.CostEstimate(
                flops=2 * height * columns * width,
                bytes_accessed=8 * height * columns + 2 * width * (height + columns),
                transcendentals=0,
            ),
        )(meta, total, *operands)

    def body(held_inverse, factor_panels, block_inverses, covariance):
        panels, tile, depth = factor_panels.shape
        sec, row = lax.axis_index("sec"), lax.axis_index("row")
        lane, mate = lax.axis_index("col") // mates, lax.axis_index("col") % mates
        block = sec * lanes + lane
        piece = tile // (secs * lanes)
        n1, n2 = sizes

        def first_second(mate):
            if not swaps:
                return sec, lane
            odd = mate % 2 == 1
            return jnp.where(odd, lane, sec), jnp.where(odd, sec, lane)

        def piece_of(mate, one, two):
            if not swaps:
                return one * lanes + two
            return jnp.where(mate % 2 == 1, two * lanes + one, one * lanes + two)

        def fence(*values):
            return lax.optimization_barrier(values)

        sub = piece // HALVES
        blocks = held_inverse.reshape(mates * HALVES * rows, 1, sub, tile)

        def share(blocks, step):
            target = (mate + step) % mates
            one, two = first_second(target)
            order = [
                (target * HALVES + h) * rows + piece_of(target, (one + a) % n1, (two + b) % n2)
                for a in range(n1)
                for b in range(n2)
                for h in range(HALVES)
            ]
            return reorder(jnp.stack(order).astype(jnp.int32), blocks).reshape(tile, tile)

        def whole_inverse(stack, name):
            part_rows = stack[None]
            for phase, size in enumerate(sizes):
                kept = part_rows
                for step in range(1, size):
                    moved = to_plane(kept, phase, step, f"{name}_plane{phase}")
                    part_rows = jnp.concatenate([part_rows, moved])
            kept = part_rows
            for step in range(1, mates):
                part_rows = jnp.concatenate([part_rows, to_mate(kept, step, f"{name}_swap")])
            ordered = []
            for q in range(rows):
                for k in range(mates):
                    one, two = first_second(k)
                    at_one, at_two = q // lanes, q % lanes
                    if swaps and k % 2:
                        at_one, at_two = at_two, at_one
                    index = (one - at_one) % n1 + (two - at_two) % n2 * n1
                    ordered.append((mate - k) % mates * rows + index)
            order = jnp.stack(ordered).astype(jnp.int32)
            return reorder(order, part_rows).reshape(rows * depth, -1)

        def sum_first(panel, factor, inverse, *held):
            scaled = scale(factor, inverse)
            scaleds = [scaled]
            scaleds += [to_mate(scaled, step, f"scaled{panel}_swap") for step in range(1, mates)]
            each = n2 * piece
            sent = product(held, scaleds, each, (n1 - 1) * each, piece, jnp.bfloat16)
            sent = sent.reshape(n1 - 1, n2, piece, -1)
            received = [
                to_plane(sent[step - 1], 0, step, f"sum{panel}_first") for step in range(1, n1)
            ]
            half_sum = product(held, scaleds, 0, each, piece, jnp.float32).reshape(n2, piece, -1)
            for value in received:
                half_sum = half_sum + value
            return half_sum

        def sum_second(panel, half_sum):
            whole_sum = half_sum[0]
            for step in range(1, n2):
                part = half_sum[step].astype(jnp.bfloat16)
                whole_sum = whole_sum + to_plane(part, 1, step, f"sum{panel}_second")
            return whole_sum.astype(jnp.bfloat16)

        def halved(own):
            return [own[h * sub : (h + 1) * sub] for h in range(HALVES)]

        def ring(panel, own):
            return jnp.stack([own] + [to_plane(own, 0, a, f"ring{panel}_first") for a in range(1, n1)])

        def ring_rest(panel, pair):
            return [pair] + [to_plane(pair, 1, b, f"ring{panel}_second") for b in range(1, n2)]

        def ring_swap(panel, lefts):
            return [
                [to_mate(value, step, f"ring{panel}_swap") for value in lefts]
                for step in range(1, mates)
            ]

        def joined(lefts, swapped):
            return sum(swapped, lefts)

        def to_columns(name, gathered):
            came = []
            for ds, dy in steps:
                target = (sec + ds) % secs * lanes + (lane + dy) % lanes

                def route(s, r, y, k):
                    return ((s + ds) % secs, r, (y + dy) % lanes, k)

                value = pick(gathered, target)
                came.append(send(value, route, f"column{name}_{ds}{dy}"))
            return came

        places = []
        for step in range(mates):
            source = (mate - step) % mates
            one, two = first_second(source)
            for b in range(n2):
                for a in range(n1):
                    place = piece_of(source, (one - a) % n1, (two - b) % n2)
                    places.append(source * tile + place * sub)
        places += [
            ((sec - ds) % secs * lanes + (lane - dy) % lanes) * sub for ds, dy in [(0, 0)] + steps
        ]
        meta = jnp.stack([row - block, mate, block, *places]).astype(jnp.int32)
        always = (row + rows) // rows == 1

        def together(function, *values):
            shapes = jax.eval_shape(function, *values)
            zeros = lambda *_: jax.tree.map(lambda x: jnp.zeros(x.shape, x.dtype), shapes)
            return lax.cond(always, function, zeros, *values)

        part = depth // (mates * rows)
        group = block * mates + mate
        own_rows = lax.dynamic_slice_in_dim(block_inverses, group * part, part, 1)

        def prepare(own_rows, blocks, factor_panels):
            stack, blocks = fence(lax.all_gather(own_rows, "row"), blocks)
            shares = [share(blocks, step) for step in range(mates)]
            held = [shares[0]] + [to_mate(shares[step], step, "held_swap") for step in range(1, mates)]
            inverses = [whole_inverse(stack[:, p], f"inverse{p}") for p in range(panels)]
            return inverses, held, [factor_panels[p] for p in range(1, panels)]

        factors = {0: lax.all_gather(factor_panels[0], "row")}
        inverses, held, waiting = together(prepare, own_rows, blocks, factor_panels)

        def both(gathered, came):
            return {h: (gathered, h * sub, came) for h in range(HALVES)}

        total, owns, pairs, moved, rests = covariance, {}, {}, {}, {}
        for now in range(panels):
            state = fence(factors, inverses, held, total, owns, pairs, moved, rests)
            factors, inverses, held, total, owns, pairs, moved, rests = state
            if now + 1 < panels:
                waiting, factors[now] = fence(waiting, factors[now])
                factors[now + 1] = lax.all_gather(waiting[now], "row")
            if now >= 1:
                moved[now - 1] = lax.all_gather(owns[now - 1], "row")
                rests[now - 1] = ring_rest(now - 1, pairs[now - 1])

            def work(factor, held, inverse, total, rest, moved):
                own = sum_second(now, sum_first(now, factor, inverse, *held))
                latest = None
                if rest is not None:
                    lefts, came = joined(rest, ring_swap(now - 2, rest)), to_columns(now - 2, moved)
                    latest = update(meta, total, lefts, both(moved, came))
                return own, halved(own), ring(now, own), latest

            owns[now], parts, pairs[now], latest = together(
                work,
                factors[now],
                held,
                inverses[now],
                total if now >= 2 else None,
                rests.get(now - 2),
                moved.get(now - 2),
            )
            if latest is not None:
                total = latest

        parts, pair, moved, rests, total = fence(parts, pairs[panels - 1], moved, rests, total)
        gathered = {0: lax.all_gather(parts[0], "row")}

        came = swapped = None
        if panels > 1:
            swapped = ring_swap(panels - 2, rests[panels - 2])
            came = together(lambda value: to_columns(panels - 2, value), moved[panels - 2])
        lefts = {}
        if panels > 1:
            lefts[panels - 2] = joined(rests[panels - 2], swapped)
        arrived = {}
        for h in range(HALVES):
            state = fence(parts, pair, moved, lefts, total, gathered, came, arrived)
            parts, pair, moved, lefts, total, gathered, came, arrived = state
            if h + 1 < HALVES:
                gathered[h + 1] = lax.all_gather(parts[h + 1], "row")
            if h == 0:

                def last_work(value, pair, total, lefts, moved, came):
                    steps_done = to_columns(f"{panels - 1}_half0", value)
                    around = ring_rest(panels - 1, pair)
                    near = ring_swap(panels - 1, [pair])
                    if came is not None:
                        total = update(meta, total, lefts, both(moved, came))
                        around, total, steps_done = fence(around, total, steps_done)
                    far = ring_swap(panels - 1, around[1:])
                    return steps_done, around[1:], near, far, total if came is not None else None

                arrived[0], rest, near, far, latest = together(
                    last_work,
                    gathered[0],
                    pair,
                    total if panels > 1 else None,
                    lefts.get(panels - 2),
                    moved.get(panels - 2),
                    came,
                )
                around = joined([pair, *rest], [one + two for one, two in zip(near, far)])
                if latest is not None:
                    total = latest
            else:
                arrived[h] = to_columns(f"{panels - 1}_half{h}", gathered[h])
                total = update(meta, total, around, {h - 1: (gathered[h - 1], 0, arrived[h - 1])})
        total = update(meta, total, around, {HALVES - 1: (gathered[HALVES - 1], 0, arrived[HALVES - 1])})
        return total

    return body


def solution(mesh):
    in_specs = (
        P("row", ("sec", "col")),
        P(None, ("sec", "col"), "row"),
        P(None, "row", None),
        P("row", ("sec", "col")),
    )
    out_specs = P("row", ("sec", "col"))
    return jax.shard_map(
        make_body(dict(mesh.shape)), mesh=mesh, in_specs=in_specs, out_specs=out_specs, check_vma=False
    )
```
